32 devices in a mesh: gx: 8 (over y, x, core), gy: 4 (over z).
Axes of the slice: x: 2, y: 2, z: 4, core: 2. Of those that a mesh axis runs over, the one named last changes fastest.
Arguments:
- features: bfloat16 [64, 64, 32, 128], P(None, 'gx', 'gy'), may hold values from -6 to 6
- cotangent: bfloat16 [64, 64, 32, 128], P(None, 'gx', 'gy'), may hold values from -6 to 6
- block_mask: int32 [8, 4, 16], P('gx', 'gy'), may hold values from 0 to 1, as said below
- kernel_one: bfloat16 [3, 3, 3, 64, 64], replicated, may hold values from -0.15625 to 0.15625
- kernel_two: bfloat16 [3, 3, 3, 64, 64], replicated, may hold values from -0.15625 to 0.15625
Outputs:
- grad_features: bfloat16 [64, 64, 32, 128], P(None, 'gx', 'gy')
- grad_one: float32 [3, 3, 3, 64, 64], replicated
- grad_two: float32 [3, 3, 3, 64, 64], replicated
The draws below stay inside these ranges and needn't reach their ends.
Inputs may be any that keep to these rules, and one draw needn't show every extreme that they name: `block_mask`: 1 marks an active block of 8 x 8 x 8 cells, 0 an empty one.
All inputs are finite; a program needn't handle non-finite values.
Results may differ from the reference program's by a relative error of at most 0.0032.
Values may be sent and summed in bfloat16 or wider, within the bound.
A program may use at most 192 MiB of HBM per device.

```python
import math
import jax
import jax.numpy as jnp
from jax import lax

C = 64
BS = 8
NX = 64
NY = 32
NZ = 128


def draw_block_mask(key, part):
    shape = (NX // BS, NY // BS, NZ // BS)
    rolls = jax.random.randint(key, shape, 0, 64)
    column = lax.broadcasted_iota(jnp.int32, shape, 0)
    limit = 24 + 36 * column // max(NX // BS - 1, 1)
    return (rolls < limit).astype(jnp.int32)


def block_levels(key, dims, split, smallest, top_value):
    gain, own = 1.0, jax.random.fold_in(key, 6)
    for axis_at, blocks in split:
        heights = jnp.exp(jax.random.uniform(jax.random.fold_in(own, axis_at), (blocks,), jnp.float32, smallest / len(split), top_value / len(split)))
        gain = gain * jnp.repeat(heights, dims[axis_at] // blocks).reshape([-1 if axis == axis_at else 1 for axis in range(len(dims))])
    return gain


def bell_draw(rng, shape, spread, bound, cuts=(), kind=jnp.bfloat16):
    drawn = spread * jax.random.normal(rng, shape, jnp.float32)
    if cuts:
        drawn = drawn * block_levels(rng, shape, cuts, -0.22, 0.18)
    return jnp.clip(drawn, -bound, bound).astype(kind)


def setup_inputs(seed: int = 0) -> dict:
    arg_keys = jax.random.split(jax.random.key(seed), 6)
    features = bell_draw(arg_keys[0], (C, NX, NY, NZ), 1.0, 6.0, ((1, 8), (2, 4)))
    cotangent = bell_draw(arg_keys[1], (C, NX, NY, NZ), 1.0, 6.0, ((1, 8), (2, 4)))
    block_mask = draw_block_mask(jax.random.fold_in(arg_keys[5], 71), 0)
    kernel_one = bell_draw(arg_keys[3], (3, 3, 3, C, C), (27 * C) ** -0.5, 0.15625)
    kernel_two = bell_draw(arg_keys[4], (3, 3, 3, C, C), (27 * C) ** -0.5, 0.15625)
    return dict(features=features, cotangent=cotangent, block_mask=block_mask, kernel_one=kernel_one, kernel_two=kernel_two)


def upsample(block_mask):
    nbx, nby, nbz = block_mask.shape
    wide = jnp.broadcast_to(block_mask[:, None, :, None, :, None], (nbx, BS, nby, BS, nbz, BS))
    return wide.reshape(nbx * BS, nby * BS, nbz * BS)

def flip_kernel(kernel):
    return jnp.transpose(jnp.flip(kernel, (0, 1, 2)), (0, 1, 2, 4, 3))

def silu_slope(value):
    sig = jax.nn.sigmoid(value)
    return sig * (1.0 + value * (1.0 - sig))

def plane_window(padded, index, width_y, width_z):
    slab = lax.dynamic_slice_in_dim(padded, index, 3, 1)
    parts = []
    for row_off in range(3):
        for col_off in range(3):
            for dep_off in range(3):
                parts.append(slab[:, row_off, col_off:col_off + width_y, dep_off:dep_off + width_z])
    return jnp.concatenate(parts, 0)

def conv_full(source, kernel):
    width_x, width_y, width_z = source.shape[1:]
    padded = jnp.pad(source.astype(jnp.float32), ((0, 0), (1, 1), (1, 1), (1, 1)))
    weights = kernel.astype(jnp.float32).reshape(27 * kernel.shape[3], kernel.shape[4])

    def plane(index):
        window = plane_window(padded, index, width_y, width_z)
        return jnp.einsum('jo,jyz->oyz', weights, window)
    planes = lax.map(plane, jnp.arange(width_x, dtype=jnp.int32))
    return jnp.transpose(planes, (1, 0, 2, 3))

def kernel_grad(source, grad):
    width_x, width_y, width_z = source.shape[1:]
    padded = jnp.pad(source.astype(jnp.float32), ((0, 0), (1, 1), (1, 1), (1, 1)))

    def plane(index):
        window = plane_window(padded, index, width_y, width_z)
        grad_plane = lax.dynamic_slice_in_dim(grad, index, 1, 1)[:, 0].astype(jnp.float32)
        return jnp.einsum('jyz,oyz->jo', window, grad_plane)
    terms = lax.map(plane, jnp.arange(width_x, dtype=jnp.int32))
    total = lax.optimization_barrier(jnp.sum(terms, 0))
    return total.reshape(3, 3, 3, source.shape[0], grad.shape[0])

def reference(features, cotangent, block_mask, kernel_one, kernel_two):
    cell = upsample(block_mask).astype(jnp.bfloat16)[None]
    cell_f = cell.astype(jnp.float32)
    masked_in = features * cell
    masked_grad = cotangent * cell
    pre_act = conv_full(masked_in, kernel_one)
    activ = (cell_f * jax.nn.silu(pre_act)).astype(jnp.bfloat16)
    act_grad = conv_full(masked_grad, flip_kernel(kernel_two))
    pre_grad = (cell_f * silu_slope(pre_act) * act_grad).astype(jnp.bfloat16)
    scale = 1.0 / math.sqrt(NX * NY * NZ)
    grad_two = kernel_grad(activ, masked_grad) * scale
    grad_one = kernel_grad(masked_in, pre_grad) * scale
    branch = conv_full(pre_grad, flip_kernel(kernel_one))
    grad_features = (cell_f * (cotangent.astype(jnp.float32) + branch)).astype(jnp.bfloat16)
    return (grad_features, grad_one, grad_two)
```

```python
import functools
import math

import jax
import jax.numpy as jnp
from jax import lax
from jax.experimental import pallas as pl
from jax.experimental.pallas import tpu as pltpu
from jax.sharding import PartitionSpec as P

BS = 8
MESH = pl.DeviceIdType.MESH
F32 = jnp.float32
BF16 = jnp.bfloat16
SCATTER = jnp.bfloat16
GATHER = jnp.float32
DIRS = ((-1, 0), (1, 0), (0, -1), (0, 1), (-1, -1), (-1, 1), (1, -1), (1, 1))


def upsample(block_mask):
    nbx, nby, nbz = block_mask.shape
    wide = jnp.broadcast_to(block_mask[:, None, :, None, :, None], (nbx, BS, nby, BS, nbz, BS))
    return wide.reshape(nbx * BS, nby * BS, nbz * BS)


def kernel(
    nx, ny, tx, ty, tz, ch, rows, scale,
    a_in, g_in, m_in, w1, w2, w3,
    out_f, out_one, out_two,
    s_a, s_g, s_h, acc, pre, act, pg,
    hx, hy, hc,
    part, part_s, rs, gyb, fin, tot,
    halo_send, halo_recv, rs_send, rs_recv, gy_send, gy_recv, ag_send, ag_recv,
):
    ix, iy = lax.axis_index("gx"), lax.axis_index("gy")
    width = ty * tz
    taps = 3 * ch

    def has(dx, dy):
        okay = None
        for pos, size, step in ((ix, nx, dx), (iy, ny, dy)):
            if step == 0:
                continue
            cond = (pos > 0) if step < 0 else (pos < size - 1)
            okay = cond if okay is None else jnp.logical_and(okay, cond)
        return okay

    barrier = pltpu.get_barrier_semaphore()
    for d in range(1, nx):
        pl.semaphore_signal(barrier, 1, device_id=(lax.rem(ix + d, nx), iy), device_id_type=MESH)
    for d in range(1, ny):
        pl.semaphore_signal(barrier, 1, device_id=(ix, lax.rem(iy + d, ny)), device_id_type=MESH)
    for dx, dy in DIRS[4:]:
        @pl.when(has(dx, dy))
        def _(dx=dx, dy=dy):
            pl.semaphore_signal(barrier, 1, device_id=(ix + dx, iy + dy), device_id_type=MESH)
    sides_x = jnp.where(ix > 0, 1, 0) + jnp.where(ix < nx - 1, 1, 0)
    sides_y = jnp.where(iy > 0, 1, 0) + jnp.where(iy < ny - 1, 1, 0)
    pl.semaphore_wait(barrier, nx + ny - 2 + sides_x * sides_y)

    def edge(source, arr, d, x0, y0):
        dx, dy = DIRS[d]
        xe = x0 if dx < 0 else x0 + tx - 1
        le = y0 * tz if dy < 0 else (y0 + ty - 1) * tz
        if dy == 0:
            src, dst = source.at[xe, :, pl.ds(y0 * tz, width)], hx.at[arr, d]
        elif dx == 0:
            src, dst = source.at[pl.ds(x0, tx), :, pl.ds(le, tz)], hy.at[arr, d - 2]
        else:
            src, dst = source.at[xe, :, pl.ds(le, tz)], hc.at[arr, d - 4]
        return pltpu.make_async_remote_copy(
            src_ref=src, dst_ref=dst,
            send_sem=halo_send.at[arr, d], recv_sem=halo_recv.at[arr, d],
            device_id=(ix + dx, iy + dy), device_id_type=MESH,
        )

    def send_halo(source, arr, x0, y0):
        for d in range(8):
            @pl.when(has(*DIRS[d]))
            def _(d=d):
                edge(source, arr, d, x0, y0).start()

    def sent_halo(source, arr, x0, y0):
        for d in range(8):
            @pl.when(has(*DIRS[d]))
            def _(d=d):
                edge(source, arr, d, x0, y0).wait_send()

    def put(stack, xp, yp, slab):
        zero = jnp.zeros((ch, 1), slab.dtype)
        at = pl.ds(yp * tz, tz)
        stack[xp, 0:ch, at] = jnp.concatenate([zero, slab[:, : tz - 1]], axis=1)
        stack[xp, ch : 2 * ch, at] = slab
        stack[xp, 2 * ch : taps, at] = jnp.concatenate([slab[:, 1:], zero], axis=1)

    def fill_inside(stack, source, x0, y0):
        def body(x, carry):
            for y in range(ty):
                put(stack, x + 1, y + 1, source[x + x0, :, (y + y0) * tz : (y + y0 + 1) * tz])
            return carry
        lax.fori_loop(0, tx, body, 0)

    def fill_halo(stack, source, arr, x0, y0):
        for d in range(8):
            dx, dy = DIRS[d]
            xp = tx + 1 if dx < 0 else 0
            yp = ty + 1 if dy < 0 else 0
            near = has(-dx, -dy)

            @pl.when(near)
            def _(d=d, dx=dx, dy=dy, xp=xp, yp=yp):
                edge(source, arr, d, x0, y0).wait_recv()
                if dy == 0:
                    for y in range(ty):
                        put(stack, xp, y + 1, hx[arr, d, :, y * tz : (y + 1) * tz])
                elif dx == 0:
                    def body(x, carry):
                        put(stack, x + 1, yp, hy[arr, d - 2, x])
                        return carry
                    lax.fori_loop(0, tx, body, 0)
                else:
                    put(stack, xp, yp, hc[arr, d - 4])

            @pl.when(jnp.logical_not(near))
            def _(dx=dx, dy=dy, xp=xp, yp=yp):
                if dy == 0:
                    stack[xp, :, pl.ds(tz, width)] = jnp.zeros((taps, width), BF16)
                elif dx == 0:
                    stack[1 : tx + 1, :, pl.ds(yp * tz, tz)] = jnp.zeros((tx, taps, tz), BF16)
                else:
                    stack[xp, :, pl.ds(yp * tz, tz)] = jnp.zeros((taps, tz), BF16)

    def conv(stack, weights, total, first, last):
        def body(xp, carry):
            window = jnp.concatenate(
                [stack[xp, :, j * tz : j * tz + width] for j in range(3)], axis=0
            )
            got = jnp.dot(weights[...], window, preferred_element_type=F32)
            for j in range(3):
                total[xp - j + 2] += got[j * ch : (j + 1) * ch]
            return carry
        lax.fori_loop(first, last, body, 0)

    def grad(local, stack, which):
        tot[...] = jnp.zeros_like(tot)

        def body(xp, carry):
            left = jnp.concatenate(
                [
                    local[xp - jx + 2, :, (2 - jy) * tz : (2 - jy + ty + 2) * tz]
                    for jx in range(3)
                    for jy in range(3)
                ],
                axis=0,
            )
            tot[...] += lax.dot_general(
                left, stack[xp], (((1,), (1,)), ((), ())), preferred_element_type=F32
            )
            return carry
        lax.fori_loop(0, tx + 2, body, 0)
        full = 9 * ch
        half = full // 2
        part[which, 0:full, :] = tot[:, 0 : 2 * ch]
        part[which, full : full + half, :] = jnp.concatenate(
            [tot[0:half, 2 * ch :], tot[half:full, 2 * ch :]], axis=1
        )
        part_s[which] = part[which].astype(SCATTER)

    def rs_copy(which, d):
        to = lax.rem(ix + d, nx)
        return pltpu.make_async_remote_copy(
            src_ref=part_s.at[which, pl.ds(to * rows, rows)], dst_ref=rs.at[which, d - 1],
            send_sem=rs_send.at[which, d - 1], recv_sem=rs_recv.at[which, d - 1],
            device_id=(to, iy), device_id_type=MESH,
        )

    def rs_start(which):
        for d in range(1, nx):
            rs_copy(which, d).start()

    def gy_copy(which, d):
        return pltpu.make_async_remote_copy(
            src_ref=gyb.at[which, iy], dst_ref=gyb.at[which, iy],
            send_sem=gy_send.at[which, d - 1], recv_sem=gy_recv.at[which, d - 1],
            device_id=(ix, lax.rem(iy + d, ny)), device_id_type=MESH,
        )

    def gy_wait(which, d):
        frm = lax.rem(iy + ny - d, ny)
        pltpu.make_async_remote_copy(
            src_ref=gyb.at[which, frm], dst_ref=gyb.at[which, frm],
            send_sem=gy_send.at[which, d - 1], recv_sem=gy_recv.at[which, d - 1],
            device_id=(ix, lax.rem(iy + d, ny)), device_id_type=MESH,
        ).wait_recv()

    def gy_start(which):
        for d in range(1, nx):
            rs_copy(which, d).wait_recv()
        total = part[which, pl.ds(pl.multiple_of(ix * rows, 8), rows)]
        for d in range(1, nx):
            total = total + rs[which, d - 1].astype(F32)
        gyb[which, iy] = total
        for d in range(1, ny):
            gy_copy(which, d).start()

    def ag_copy(which, d):
        return pltpu.make_async_remote_copy(
            src_ref=fin.at[which, ix], dst_ref=fin.at[which, ix],
            send_sem=ag_send.at[which, d - 1], recv_sem=ag_recv.at[which, d - 1],
            device_id=(lax.rem(ix + d, nx), iy), device_id_type=MESH,
        )

    def ag_wait(which, d):
        frm = lax.rem(ix + nx - d, nx)
        pltpu.make_async_remote_copy(
            src_ref=fin.at[which, frm], dst_ref=fin.at[which, frm],
            send_sem=ag_send.at[which, d - 1], recv_sem=ag_recv.at[which, d - 1],
            device_id=(lax.rem(ix + d, nx), iy), device_id_type=MESH,
        ).wait_recv()

    def ag_start(which):
        for d in range(1, ny):
            gy_wait(which, d)
        total = gyb[which, 0]
        for d in range(1, ny):
            total = total + gyb[which, d]
        fin[which, ix] = (total * scale).astype(GATHER)
        for d in range(1, nx):
            ag_copy(which, d).start()

    def finish(which, out):
        for d in range(1, nx):
            ag_wait(which, d)
        half = 9 * ch // 2
        flat = fin[which].astype(F32).reshape(nx * rows, 2 * ch)
        for j in range(9):
            block = flat[j * ch : (j + 1) * ch]
            lo = j * ch
            for k in range(2):
                emit(which, out, j, k, block[:, k * ch : (k + 1) * ch])
            if lo + ch <= half:
                tail = flat[9 * ch + lo : 9 * ch + lo + ch, 0:ch]
            elif lo >= half:
                tail = flat[9 * ch + lo - half : 9 * ch + lo - half + ch, ch:]
            else:
                cut = half - lo
                tail = jnp.concatenate(
                    [flat[9 * ch + lo : 9 * ch + half, 0:ch], flat[9 * ch : 10 * ch - cut, ch:]], axis=0
                )
            emit(which, out, j, 2, tail)

    def emit(which, out, j, k, block):
        jx, jy = j // 3, j % 3
        if which == 0:
            out[2 - jx, 2 - jy, 2 - k] = block
        else:
            out[jx, jy, k] = jnp.transpose(block)

    send_halo(a_in, 0, 0, 0)
    send_halo(g_in, 1, 0, 0)

    for pad in (act, pg):
        for x in (0, 1, tx + 2, tx + 3):
            pad[x] = jnp.zeros(pad.shape[1:], BF16)
        pad[:, :, 0 : 2 * tz] = jnp.zeros((tx + 4, ch, 2 * tz), BF16)
        pad[:, :, 2 * tz + width :] = jnp.zeros((tx + 4, ch, 2 * tz), BF16)
    part[:, 27 * ch // 2 :, :] = jnp.zeros((2, nx * rows - 27 * ch // 2, 2 * ch), F32)
    pre[...] = jnp.zeros_like(pre)
    acc[...] = jnp.zeros_like(acc)

    fill_inside(s_a, a_in, 0, 0)
    fill_inside(s_g, g_in, 0, 0)
    fill_halo(s_a, a_in, 0, 0, 0)
    conv(s_a, w1, pre, 0, tx + 2)
    fill_halo(s_g, g_in, 1, 0, 0)
    conv(s_g, w2, acc, 0, tx + 2)

    def middle(x, carry):
        value = pre[x + 2]
        mask = m_in[x]
        sig = jax.nn.sigmoid(value)
        act[x + 2, :, 2 * tz : 2 * tz + width] = (mask * (value * sig)).astype(BF16)
        slope = sig * (1.0 + value * (1.0 - sig))
        pg[x + 2, :, 2 * tz : 2 * tz + width] = (mask * slope * acc[x + 2]).astype(BF16)
        return carry
    lax.fori_loop(0, tx, middle, 0)
    send_halo(pg, 2, 2, 2)
    grad(act, s_g, 0)
    rs_start(0)
    grad(pg, s_a, 1)
    rs_start(1)
    acc[...] = jnp.zeros_like(acc)
    fill_inside(s_h, pg, 2, 2)
    gy_start(0)
    fill_halo(s_h, pg, 2, 2, 2)
    mid = (tx + 2) // 2
    conv(s_h, w3, acc, 0, mid)
    gy_start(1)
    ag_start(0)
    conv(s_h, w3, acc, mid, tx + 2)
    ag_start(1)

    def ending(x, carry):
        out_f[x] = (g_in[x].astype(F32) + m_in[x] * acc[x + 2]).astype(BF16)
        return carry
    lax.fori_loop(0, tx, ending, 0)
    finish(0, out_two)
    finish(1, out_one)
    sent_halo(a_in, 0, 0, 0)
    sent_halo(g_in, 1, 0, 0)
    sent_halo(pg, 2, 2, 2)
    for which in range(2):
        for d in range(1, nx):
            rs_copy(which, d).wait_send()
            ag_copy(which, d).wait_send()
        for d in range(1, ny):
            gy_copy(which, d).wait_send()


def shards(features, cotangent, block_mask, kernel_one, kernel_two):
    ch, tx, ty, tz = features.shape
    nx, ny = lax.axis_size("gx"), lax.axis_size("gy")
    width = ty * tz
    cell = upsample(block_mask)
    cell_b = cell.astype(BF16)[None]
    a_in = jnp.transpose(features * cell_b, (1, 0, 2, 3)).reshape(tx, ch, width)
    g_in = jnp.transpose(cotangent * cell_b, (1, 0, 2, 3)).reshape(tx, ch, width)
    m_in = cell.astype(F32).reshape(tx, 1, width)
    w1 = jnp.transpose(kernel_one, (0, 4, 1, 2, 3)).reshape(3 * ch, 9 * ch)
    w2 = jnp.transpose(jnp.flip(kernel_two, (0, 1, 2)), (0, 3, 1, 2, 4)).reshape(3 * ch, 9 * ch)
    w3 = jnp.transpose(jnp.flip(kernel_one, (0, 1, 2)), (0, 3, 1, 2, 4)).reshape(3 * ch, 9 * ch)
    need = -(-(27 * ch // 2) // nx)
    rows = -(-need // 16) * 16
    scale = 1.0 / math.sqrt(tx * ty * tz * nx * ny)
    vm = pl.BlockSpec(memory_space=pltpu.VMEM)
    dma = pltpu.SemaphoreType.DMA
    stack = pltpu.VMEM((tx + 2, 3 * ch, (ty + 2) * tz), BF16)
    total = pltpu.VMEM((tx + 4, ch, width), F32)
    pad = pltpu.VMEM((tx + 4, ch, (ty + 4) * tz), BF16)
    out_f, out_one, out_two = pl.pallas_call(
        functools.partial(kernel, nx, ny, tx, ty, tz, ch, rows, scale),
        out_shape=(
            jax.ShapeDtypeStruct((tx, ch, width), BF16),
            jax.ShapeDtypeStruct((3, 3, 3, ch, ch), F32),
            jax.ShapeDtypeStruct((3, 3, 3, ch, ch), F32),
        ),
        in_specs=[vm] * 6,
        out_specs=(vm, vm, vm),
        scratch_shapes=[
            stack, stack, stack, total, total, pad, pad,
            pltpu.VMEM((3, 2, ch, width), BF16),
            pltpu.VMEM((3, 2, tx, ch, tz), BF16),
            pltpu.VMEM((3, 4, ch, tz), BF16),
            pltpu.VMEM((2, nx * rows, 2 * ch), F32),
            pltpu.VMEM((2, nx * rows, 2 * ch), SCATTER),
            pltpu.VMEM((2, nx - 1, rows, 2 * ch), SCATTER),
            pltpu.VMEM((2, ny, rows, 2 * ch), F32),
            pltpu.VMEM((2, nx, rows, 2 * ch), GATHER),
            pltpu.VMEM((9 * ch, 3 * ch), F32),
            dma((3, 8)), dma((3, 8)),
            dma((2, nx - 1)), dma((2, nx - 1)),
            dma((2, ny - 1)), dma((2, ny - 1)),
            dma((2, nx - 1)), dma((2, nx - 1)),
        ],
        compiler_params=pltpu.CompilerParams(
            collective_id=0, has_side_effects=True, vmem_limit_bytes=56 * 2**20
        ),
    )(a_in, g_in, m_in, w1, w2, w3)
    grad_features = jnp.transpose(out_f.reshape(tx, ch, ty, tz), (1, 0, 2, 3))
    return (grad_features, out_one, out_two)


def solution(mesh):
    placed = (P(None, "gx", "gy", None), P(None, "gx", "gy", None), P("gx", "gy", None), P(), P())
    return jax.shard_map(
        shards,
        mesh=mesh,
        in_specs=placed,
        out_specs=(P(None, "gx", "gy", None), P(), P()),
        check_vma=False,
    )
```

```python
import functools
import math

import jax
import jax.numpy as jnp
from jax import lax
from jax.experimental import pallas as pl
from jax.experimental.pallas import tpu as pltpu
from jax.sharding import PartitionSpec as P

BS = 8
MESH = pl.DeviceIdType.MESH
F32 = jnp.float32
BF16 = jnp.bfloat16
SCATTER = jnp.bfloat16
GATHER = jnp.bfloat16
DIRS = ((-1, 0), (1, 0), (0, -1), (0, 1), (-1, -1), (-1, 1), (1, -1), (1, 1))


def upsample(block_mask):
    nbx, nby, nbz = block_mask.shape
    wide = jnp.broadcast_to(block_mask[:, None, :, None, :, None], (nbx, BS, nby, BS, nbz, BS))
    return wide.reshape(nbx * BS, nby * BS, nbz * BS)


def kernel(
    nx, ny, tx, ty, tz, ch, rows, scale,
    a_in, g_in, m_in, k1, k2,
    out_f, out_one, out_two,
    s_a, s_g, s_h, acc, pre, act, pg,
    hx, hy, hc,
    part, part_s, rs, csum, gsl, fin, tot, w1, w2, w3,
    halo_send, halo_recv, rs_send, rs_recv, gy_send, gy_recv, ag_send, ag_recv,
):
    ix, iy = lax.axis_index("gx"), lax.axis_index("gy")
    width = ty * tz
    taps = 3 * ch

    def has(dx, dy):
        okay = None
        for pos, size, step in ((ix, nx, dx), (iy, ny, dy)):
            if step == 0:
                continue
            cond = (pos > 0) if step < 0 else (pos < size - 1)
            okay = cond if okay is None else jnp.logical_and(okay, cond)
        return okay

    barrier = pltpu.get_barrier_semaphore()
    for d in range(1, nx):
        pl.semaphore_signal(barrier, 1, device_id=(lax.rem(ix + d, nx), iy), device_id_type=MESH)
    for d in range(1, ny):
        pl.semaphore_signal(barrier, 1, device_id=(ix, lax.rem(iy + d, ny)), device_id_type=MESH)
    for dx, dy in DIRS[4:]:
        @pl.when(has(dx, dy))
        def _(dx=dx, dy=dy):
            pl.semaphore_signal(barrier, 1, device_id=(ix + dx, iy + dy), device_id_type=MESH)
    sides_x = jnp.where(ix > 0, 1, 0) + jnp.where(ix < nx - 1, 1, 0)
    sides_y = jnp.where(iy > 0, 1, 0) + jnp.where(iy < ny - 1, 1, 0)
    pl.semaphore_wait(barrier, nx + ny - 2 + sides_x * sides_y)

    def edge(source, arr, d, x0, y0):
        dx, dy = DIRS[d]
        xe = x0 if dx < 0 else x0 + tx - 1
        le = y0 * tz if dy < 0 else (y0 + ty - 1) * tz
        if dy == 0:
            src, dst = source.at[xe, :, pl.ds(y0 * tz, width)], hx.at[arr, d]
        elif dx == 0:
            src, dst = source.at[pl.ds(x0, tx), :, pl.ds(le, tz)], hy.at[arr, d - 2]
        else:
            src, dst = source.at[xe, :, pl.ds(le, tz)], hc.at[arr, d - 4]
        return pltpu.make_async_remote_copy(
            src_ref=src, dst_ref=dst,
            send_sem=halo_send.at[arr, d], recv_sem=halo_recv.at[arr, d],
            device_id=(ix + dx, iy + dy), device_id_type=MESH,
        )

    def send_halo(source, arr, x0, y0):
        for d in range(8):
            @pl.when(has(*DIRS[d]))
            def _(d=d):
                edge(source, arr, d, x0, y0).start()

    def sent_halo(source, arr, x0, y0):
        for d in range(8):
            @pl.when(has(*DIRS[d]))
            def _(d=d):
                edge(source, arr, d, x0, y0).wait_send()

    def put(stack, xp, yp, slab):
        zero = jnp.zeros((ch, 1), slab.dtype)
        at = pl.ds(yp * tz, tz)
        stack[xp, 0:ch, at] = jnp.concatenate([zero, slab[:, : tz - 1]], axis=1)
        stack[xp, ch : 2 * ch, at] = slab
        stack[xp, 2 * ch : taps, at] = jnp.concatenate([slab[:, 1:], zero], axis=1)

    def fill_inside(stack, source, x0, y0):
        def body(x, carry):
            for y in range(ty):
                put(stack, x + 1, y + 1, source[x + x0, :, (y + y0) * tz : (y + y0 + 1) * tz])
            return carry
        lax.fori_loop(0, tx, body, 0)

    def fill_halo(stack, source, arr, x0, y0):
        for d in range(8):
            dx, dy = DIRS[d]
            xp = tx + 1 if dx < 0 else 0
            yp = ty + 1 if dy < 0 else 0
            near = has(-dx, -dy)

            @pl.when(near)
            def _(d=d, dx=dx, dy=dy, xp=xp, yp=yp):
                edge(source, arr, d, x0, y0).wait_recv()
                if dy == 0:
                    for y in range(ty):
                        put(stack, xp, y + 1, hx[arr, d, :, y * tz : (y + 1) * tz])
                elif dx == 0:
                    def body(x, carry):
                        put(stack, x + 1, yp, hy[arr, d - 2, x])
                        return carry
                    lax.fori_loop(0, tx, body, 0)
                else:
                    put(stack, xp, yp, hc[arr, d - 4])

            @pl.when(jnp.logical_not(near))
            def _(dx=dx, dy=dy, xp=xp, yp=yp):
                if dy == 0:
                    stack[xp, :, pl.ds(tz, width)] = jnp.zeros((taps, width), BF16)
                elif dx == 0:
                    stack[1 : tx + 1, :, pl.ds(yp * tz, tz)] = jnp.zeros((tx, taps, tz), BF16)
                else:
                    stack[xp, :, pl.ds(yp * tz, tz)] = jnp.zeros((taps, tz), BF16)

    def conv(stack, weights, total, first, last):
        def body(xp, carry):
            window = jnp.concatenate(
                [stack[xp, :, j * tz : j * tz + width] for j in range(3)], axis=0
            )
            got = jnp.dot(weights[...], window, preferred_element_type=F32)
            for j in range(3):
                total[xp - j + 2] += got[j * ch : (j + 1) * ch]
            return carry
        lax.fori_loop(first, last, body, 0)

    def grad(local, stack, which):
        tot[...] = jnp.zeros_like(tot)

        def body(xp, carry):
            left = jnp.concatenate(
                [
                    local[xp - jx + 2, :, (2 - jy) * tz : (2 - jy + ty + 2) * tz]
                    for jx in range(3)
                    for jy in range(3)
                ],
                axis=0,
            )
            tot[...] += lax.dot_general(
                left, stack[xp], (((1,), (1,)), ((), ())), preferred_element_type=F32
            )
            return carry
        lax.fori_loop(0, tx + 2, body, 0)
        full = 9 * ch
        half = full // 2
        part[which, 0:full, :] = tot[:, 0 : 2 * ch]
        part[which, full : full + half, :] = jnp.concatenate(
            [tot[0:half, 2 * ch :], tot[half:full, 2 * ch :]], axis=1
        )
        part_s[which] = part[which].astype(SCATTER)

    def rs_copy(which, d):
        to = lax.rem(ix + d, nx)
        return pltpu.make_async_remote_copy(
            src_ref=part_s.at[which, pl.ds(to * rows, rows)], dst_ref=rs.at[which, d - 1],
            send_sem=rs_send.at[which, d - 1], recv_sem=rs_recv.at[which, d - 1],
            device_id=(to, iy), device_id_type=MESH,
        )

    def rs_start(which):
        for d in range(1, nx):
            rs_copy(which, d).start()

    sub = rows // ny

    def gs_copy(which, d):
        to = lax.rem(iy + d, ny)
        return pltpu.make_async_remote_copy(
            src_ref=csum.at[which, pl.ds(to * sub, sub)], dst_ref=gsl.at[which, d - 1],
            send_sem=gy_send.at[which, d - 1], recv_sem=gy_recv.at[which, d - 1],
            device_id=(ix, to), device_id_type=MESH,
        )

    def gg_copy(which, d, owner):
        mine = fin.at[which, ix, pl.ds(owner * sub, sub)]
        return pltpu.make_async_remote_copy(
            src_ref=mine, dst_ref=mine,
            send_sem=gy_send.at[which + 2, d - 1], recv_sem=gy_recv.at[which + 2, d - 1],
            device_id=(ix, lax.rem(iy + d, ny)), device_id_type=MESH,
        )

    def gs_start(which):
        for d in range(1, nx):
            rs_copy(which, d).wait_recv()
        total = part[which, pl.ds(pl.multiple_of(ix * rows, 16), rows)]
        for d in range(1, nx):
            total = total + rs[which, d - 1].astype(F32)
        csum[which] = total
        for d in range(1, ny):
            gs_copy(which, d).start()

    def gg_start(which):
        for d in range(1, ny):
            gs_copy(which, d).wait_recv()
        at = pl.ds(pl.multiple_of(iy * sub, 16), sub)
        total = csum[which, at]
        for d in range(1, ny):
            total = total + gsl[which, d - 1]
        fin[which, ix, at] = (total * scale).astype(GATHER)
        for d in range(1, ny):
            gg_copy(which, d, iy).start()

    def ag_copy(which, d):
        return pltpu.make_async_remote_copy(
            src_ref=fin.at[which, ix], dst_ref=fin.at[which, ix],
            send_sem=ag_send.at[which, d - 1], recv_sem=ag_recv.at[which, d - 1],
            device_id=(lax.rem(ix + d, nx), iy), device_id_type=MESH,
        )

    def ag_wait(which, d):
        frm = lax.rem(ix + nx - d, nx)
        pltpu.make_async_remote_copy(
            src_ref=fin.at[which, frm], dst_ref=fin.at[which, frm],
            send_sem=ag_send.at[which, d - 1], recv_sem=ag_recv.at[which, d - 1],
            device_id=(lax.rem(ix + d, nx), iy), device_id_type=MESH,
        ).wait_recv()

    def ag_start(which):
        for d in range(1, ny):
            gg_copy(which, d, lax.rem(iy + ny - d, ny)).wait_recv()
        for d in range(1, nx):
            ag_copy(which, d).start()

    def finish(which, out):
        for d in range(1, nx):
            ag_wait(which, d)
        half = 9 * ch // 2
        flat = fin[which].astype(F32).reshape(nx * rows, 2 * ch)
        for j in range(9):
            block = flat[j * ch : (j + 1) * ch]
            lo = j * ch
            for k in range(2):
                emit(which, out, j, k, block[:, k * ch : (k + 1) * ch])
            if lo + ch <= half:
                tail = flat[9 * ch + lo : 9 * ch + lo + ch, 0:ch]
            elif lo >= half:
                tail = flat[9 * ch + lo - half : 9 * ch + lo - half + ch, ch:]
            else:
                cut = half - lo
                tail = jnp.concatenate(
                    [flat[9 * ch + lo : 9 * ch + half, 0:ch], flat[9 * ch : 10 * ch - cut, ch:]], axis=0
                )
            emit(which, out, j, 2, tail)

    def emit(which, out, j, k, block):
        jx, jy = j // 3, j % 3
        if which == 0:
            out[2 - jx, 2 - jy, 2 - k] = block
        else:
            out[jx, jy, k] = jnp.transpose(block)

    send_halo(a_in, 0, 0, 0)
    send_halo(g_in, 1, 0, 0)

    for pad in (act, pg):
        for x in (0, 1, tx + 2, tx + 3):
            pad[x] = jnp.zeros(pad.shape[1:], BF16)
        pad[:, :, 0 : 2 * tz] = jnp.zeros((tx + 4, ch, 2 * tz), BF16)
        pad[:, :, 2 * tz + width :] = jnp.zeros((tx + 4, ch, 2 * tz), BF16)
    part[:, 27 * ch // 2 :, :] = jnp.zeros((2, nx * rows - 27 * ch // 2, 2 * ch), F32)
    pre[...] = jnp.zeros_like(pre)
    acc[...] = jnp.zeros_like(acc)

    for jx in range(3):
        low = jx * ch
        for n in range(0, 9, 2):
            these = [jx * 9 + m for m in range(n, min(n + 2, 9))]
            cols = slice(n * ch, (n + len(these)) * ch)
            w1[low : low + ch, cols] = jnp.transpose(jnp.concatenate([k1[t] for t in these], axis=0))
            w2[low : low + ch, cols] = jnp.concatenate([k2[26 - t] for t in these], axis=1)
            w3[low : low + ch, cols] = jnp.concatenate([k1[26 - t] for t in these], axis=1)

    fill_inside(s_a, a_in, 0, 0)
    fill_inside(s_g, g_in, 0, 0)
    fill_halo(s_a, a_in, 0, 0, 0)
    conv(s_a, w1, pre, 0, tx + 2)

    def middle(x, carry):
        value = pre[x + 2]
        mask = m_in[x]
        sig = jax.nn.sigmoid(value)
        act[x + 2, :, 2 * tz : 2 * tz + width] = (mask * (value * sig)).astype(BF16)
        pre[x + 2] = mask * (sig * (1.0 + value * (1.0 - sig)))
        return carry
    lax.fori_loop(0, tx, middle, 0)
    fill_halo(s_g, g_in, 1, 0, 0)
    grad(act, s_g, 0)
    rs_start(0)
    conv(s_g, w2, acc, 0, tx + 2)

    def after(x, carry):
        pg[x + 2, :, 2 * tz : 2 * tz + width] = (pre[x + 2] * acc[x + 2]).astype(BF16)
        return carry
    lax.fori_loop(0, tx, after, 0)
    send_halo(pg, 2, 2, 2)
    gs_start(0)
    grad(pg, s_a, 1)
    rs_start(1)
    gg_start(0)
    acc[...] = jnp.zeros_like(acc)
    fill_inside(s_h, pg, 2, 2)
    ag_start(0)
    fill_halo(s_h, pg, 2, 2, 2)
    cuts = [(tx + 2) * k // 5 for k in (0, 2, 4, 5)]
    conv(s_h, w3, acc, cuts[0], cuts[1])
    gs_start(1)
    conv(s_h, w3, acc, cuts[1], cuts[2])
    gg_start(1)
    conv(s_h, w3, acc, cuts[2], cuts[3])
    ag_start(1)

    def ending(x, carry):
        out_f[x] = (g_in[x].astype(F32) + m_in[x] * acc[x + 2]).astype(BF16)
        return carry
    lax.fori_loop(0, tx, ending, 0)
    finish(0, out_two)
    finish(1, out_one)
    sent_halo(a_in, 0, 0, 0)
    sent_halo(g_in, 1, 0, 0)
    sent_halo(pg, 2, 2, 2)
    for which in range(2):
        for d in range(1, nx):
            rs_copy(which, d).wait_send()
            ag_copy(which, d).wait_send()
        for d in range(1, ny):
            gs_copy(which, d).wait_send()
            gg_copy(which, d, iy).wait_send()


def shards(features, cotangent, block_mask, kernel_one, kernel_two):
    ch, tx, ty, tz = features.shape
    nx, ny = lax.axis_size("gx"), lax.axis_size("gy")
    width = ty * tz
    cell = upsample(block_mask)
    cell_b = cell.astype(BF16)[None]
    a_in = jnp.transpose(features * cell_b, (1, 0, 2, 3)).reshape(tx, ch, width)
    g_in = jnp.transpose(cotangent * cell_b, (1, 0, 2, 3)).reshape(tx, ch, width)
    m_in = cell.astype(F32).reshape(tx, 1, width)
    k1 = kernel_one.reshape(27, ch, ch)
    k2 = kernel_two.reshape(27, ch, ch)
    need = -(-(27 * ch // 2) // nx)
    rows = -(-need // (16 * ny)) * 16 * ny
    sub = rows // ny
    scale = 1.0 / math.sqrt(tx * ty * tz * nx * ny)
    weight = pltpu.VMEM((3 * ch, 9 * ch), BF16)
    vm = pl.BlockSpec(memory_space=pltpu.VMEM)
    dma = pltpu.SemaphoreType.DMA
    stack = pltpu.VMEM((tx + 2, 3 * ch, (ty + 2) * tz), BF16)
    total = pltpu.VMEM((tx + 4, ch, width), F32)
    pad = pltpu.VMEM((tx + 4, ch, (ty + 4) * tz), BF16)
    out_f, out_one, out_two = pl.pallas_call(
        functools.partial(kernel, nx, ny, tx, ty, tz, ch, rows, scale),
        out_shape=(
            jax.ShapeDtypeStruct((tx, ch, width), BF16),
            jax.ShapeDtypeStruct((3, 3, 3, ch, ch), F32),
            jax.ShapeDtypeStruct((3, 3, 3, ch, ch), F32),
        ),
        in_specs=[vm] * 5,
        out_specs=(vm, vm, vm),
        scratch_shapes=[
            stack, stack, stack, total, total, pad, pad,
            pltpu.VMEM((3, 2, ch, width), BF16),
            pltpu.VMEM((3, 2, tx, ch, tz), BF16),
            pltpu.VMEM((3, 4, ch, tz), BF16),
            pltpu.VMEM((2, nx * rows, 2 * ch), F32),
            pltpu.VMEM((2, nx * rows, 2 * ch), SCATTER),
            pltpu.VMEM((2, nx - 1, rows, 2 * ch), SCATTER),
            pltpu.VMEM((2, rows, 2 * ch), F32),
            pltpu.VMEM((2, ny - 1, sub, 2 * ch), F32),
            pltpu.VMEM((2, nx, rows, 2 * ch), GATHER),
            pltpu.VMEM((9 * ch, 3 * ch), F32),
            weight, weight, weight,
            dma((3, 8)), dma((3, 8)),
            dma((2, nx - 1)), dma((2, nx - 1)),
            dma((4, ny - 1)), dma((4, ny - 1)),
            dma((2, nx - 1)), dma((2, nx - 1)),
        ],
        compiler_params=pltpu.CompilerParams(
            collective_id=0, has_side_effects=True, vmem_limit_bytes=56 * 2**20
        ),
    )(a_in, g_in, m_in, k1, k2)
    grad_features = jnp.transpose(out_f.reshape(tx, ch, ty, tz), (1, 0, 2, 3))
    return (grad_features, out_one, out_two)


def solution(mesh):
    placed = (P(None, "gx", "gy", None), P(None, "gx", "gy", None), P("gx", "gy", None), P(), P())
    return jax.shard_map(
        shards,
        mesh=mesh,
        in_specs=placed,
        out_specs=(P(None, "gx", "gy", None), P(), P()),
        check_vma=False,
    )
```
